256 devices in a mesh: dp: 64 (over y_hi, z, x), tensor: 4 (over y_lo, core).
Axes of the slice: x: 4, y: 4 (y_hi: 2, y_lo: 2; y = y_hi * 2 + y_lo), z: 8, core: 2. Of those that a mesh axis runs over, the one named last changes fastest.
Arguments:
- image_feats: bfloat16 [12288, 1152], P('dp', 'tensor'), may hold values from -6 to 6
- text_feats: bfloat16 [12288, 1152], P('dp', 'tensor'), may hold values from -6 to 6
- image_proj: bfloat16 [1152, 1152], P('tensor'), may hold values from -0.1875 to 0.1875
- text_proj: bfloat16 [1152, 1152], P('tensor'), may hold values from -0.1875 to 0.1875
Outputs:
- grad_image_feats: bfloat16 [12288, 1152], P('dp', 'tensor')
- grad_text_feats: bfloat16 [12288, 1152], P('dp', 'tensor')
- grad_image_proj: float32 [1152, 1152], P('tensor')
- text_head_gradient: float32 [1152, 1152], P('tensor')
The draws below stay inside these ranges and needn't reach their ends.
All inputs are finite; a program needn't handle non-finite values.
Results may differ from the reference program's by a relative error of at most 0.02.
Values may be sent and summed in bfloat16 or wider, within the bound.
No kernel may reach another device: no remote copies, remote signals or barrier semaphores. Data moves between devices by JAX's collectives and lax.ppermute only.
A program may use at most 64 MiB of HBM per device.

```python
import jax
import jax.numpy as jnp
from jax import lax

D = 1152
E = 1152
PAIRS_DEV = 192
PAIRS = 12288


def block_levels(key, extent, cuts, least, top_value):
    factor_of = 1.0
    for position, shards_of in cuts:
        steps = jax.random.uniform(jax.random.fold_in(jax.random.fold_in(key, 6), position), (shards_of,), jnp.float32, least / len(cuts), top_value / len(cuts))
        factor_of = factor_of * jnp.repeat(jnp.exp(steps), extent[position] // shards_of).reshape((-1,) + (1,) * (len(extent) - 1 - position))
    return factor_of


def centred(key, extent, spread, bound, shards=(), kind=jnp.bfloat16):
    result = jax.random.normal(key, extent, jnp.float32) * spread
    if len(shards) > 0:
        result = block_levels(key, extent, shards, -0.22, 0.18) * result
    return jnp.clip(result, min=-bound, max=bound).astype(kind)


def setup_inputs(seed: int = 0) -> dict:
    arg_keys = jax.random.split(jax.random.key(seed), 5)
    image_feats = centred(arg_keys[0], (PAIRS, D), 1.0, 6.0, ((0, 64), (1, 4)))
    text_feats = centred(arg_keys[1], (PAIRS, D), 1.0, 6.0, ((0, 64), (1, 4)))
    image_proj = centred(arg_keys[2], (D, E), D ** -0.5, 0.1875, ((0, 4),))
    text_proj = centred(arg_keys[3], (D, E), D ** -0.5, 0.1875, ((0, 4),))
    return dict(image_feats=image_feats, text_feats=text_feats, image_proj=image_proj, text_proj=text_proj)


SOFTNESS_SCALE = 10.0
SCORE_OFFSET_BIAS = -4.0
EPSILON = 1e-06

def normalize(raw):
    radius = jnp.sqrt(lax.optimization_barrier(jnp.sum(raw * raw, axis=1, keepdims=True)) + EPSILON)
    return (raw / radius, radius)

def backnorm(unit, radius, grad):
    return ((grad - unit * lax.optimization_barrier(jnp.sum(unit * grad, axis=1, keepdims=True))) / radius).astype(jnp.bfloat16)

def reference(image_feats, text_feats, image_proj, text_proj):
    image_raw = jnp.dot(image_feats, image_proj, preferred_element_type=jnp.float32)
    text_raw = jnp.dot(text_feats, text_proj, preferred_element_type=jnp.float32)
    image_unit, image_radius = normalize(image_raw)
    text_unit, text_radius = normalize(text_raw)
    image_emb = image_unit.astype(jnp.bfloat16)
    text_emb = text_unit.astype(jnp.bfloat16)
    col_ids = jnp.arange(PAIRS, dtype=jnp.int32)
    row_iota = jnp.arange(PAIRS_DEV, dtype=jnp.int32)

    def block_step(text_total, index):
        start = (index * PAIRS_DEV).astype(jnp.int32)
        image_block = lax.dynamic_slice_in_dim(image_emb, start, PAIRS_DEV, 0)
        pair_scores = lax.dot_general(image_block, text_emb, (((1,), (1,)), ((), ())), preferred_element_type=jnp.float32)
        pair_logit_values = SOFTNESS_SCALE * pair_scores + SCORE_OFFSET_BIAS
        match_label = ((start + row_iota)[:, None] == col_ids[None, :]).astype(jnp.float32)
        loss_weights = (SOFTNESS_SCALE * (jax.nn.sigmoid(pair_logit_values) - match_label)).astype(jnp.bfloat16)
        image_grad = jnp.dot(loss_weights, text_emb, preferred_element_type=jnp.float32)
        text_total = text_total + lax.dot_general(loss_weights, image_block, (((0,), (0,)), ((), ())), preferred_element_type=jnp.float32)
        return (text_total, image_grad)
    text_init = jnp.zeros((PAIRS, E), jnp.float32)
    grad_text_emb, image_blocks = lax.scan(block_step, text_init, jnp.arange(PAIRS // PAIRS_DEV, dtype=jnp.int32))
    grad_image_emb = image_blocks.reshape(PAIRS, E)
    image_grad_raw = backnorm(image_unit, image_radius, grad_image_emb)
    text_grad_raw = backnorm(text_unit, text_radius, grad_text_emb)
    grad_image_feats = jnp.dot(image_grad_raw, image_proj.T, preferred_element_type=jnp.float32).astype(jnp.bfloat16)
    grad_text_feats = jnp.dot(text_grad_raw, text_proj.T, preferred_element_type=jnp.float32).astype(jnp.bfloat16)
    grad_image_proj = jnp.dot(image_feats.T, image_grad_raw, preferred_element_type=jnp.float32)
    text_head_gradient = jnp.dot(text_feats.T, text_grad_raw, preferred_element_type=jnp.float32)
    return (grad_image_feats, grad_text_feats, grad_image_proj, text_head_gradient)
```

```python
import jax
import jax.numpy as jnp
from jax import lax
from jax.sharding import Mesh, PartitionSpec as P

SCALE = 10.0
OFFSET = -4.0
EPSILON = 1e-06
F32 = jnp.float32
BF16 = jnp.bfloat16

AXES = ("yhi", "z", "x", "ylo", "core")
PLANE = ("yhi", "x", "ylo")
TENSOR = ("ylo", "core")
LANES = 128


def shift(value, axis, by):
    n = lax.axis_size(axis)
    return lax.ppermute(value, axis, [(i, (i + by) % n) for i in range(n)])


def flip(value, axis, bit):
    n = lax.axis_size(axis)
    return lax.ppermute(value, axis, [(i, i ^ bit) for i in range(n)])


def broadcast_gather(value, axes, members):
    return lax.all_to_all(jnp.broadcast_to(value[None], (members,) + value.shape), axes, 0, 0)


def normalize(raw):
    radius = jnp.sqrt(jnp.sum(raw * raw, axis=1, keepdims=True) + EPSILON)
    return (raw / radius, radius)


def backnorm(unit, radius, grad):
    return ((grad - unit * jnp.sum(unit * grad, axis=1, keepdims=True)) / radius).astype(BF16)


def head_rows(partial):
    core, ylo = lax.axis_index("core"), lax.axis_index("ylo")
    rows, width = partial.shape
    parts = partial.reshape(2, 2, rows // 4, width)
    keep = lax.dynamic_index_in_dim(parts, core, 1, keepdims=False)
    send = lax.dynamic_index_in_dim(parts, 1 - core, 1, keepdims=False)
    half = keep + flip(send.astype(BF16), "core", 1).astype(F32)
    keep = lax.dynamic_index_in_dim(half, ylo, 0, keepdims=False)
    send = lax.dynamic_index_in_dim(half, 1 - ylo, 0, keepdims=False)
    return keep + flip(send.astype(BF16), "ylo", 1).astype(F32)


def ring_gather(value):
    up = down = value
    out = [value]
    for step in range(4):
        up = shift(up, "z", 1)
        out.append(up)
        if step < 3:
            down = shift(down, "z", -1)
            out.append(down)
    return jnp.concatenate(out, axis=0)


def ring_sum(parts):
    part = {0: 0, -1: 1, 1: 2, -2: 3, 2: 4, -3: 5, 3: 6, -4: 7}
    down = shift(parts[part[-4]].astype(BF16), "z", -1)
    up = shift(parts[part[3]].astype(BF16), "z", 1)
    for step in (3, 2, 1):
        down = shift((parts[part[-step]] + down.astype(F32)).astype(BF16), "z", -1)
        if step > 1:
            up = shift((parts[part[step - 1]] + up.astype(F32)).astype(BF16), "z", 1)
    return parts[part[0]] + down.astype(F32) + up.astype(F32)


def to_lanes(grad, pieces, unit):
    rows, width = grad.shape
    flat = grad.reshape(rows, width // LANES, LANES).transpose(1, 0, 2).reshape(-1, LANES)
    return jnp.pad(flat, ((0, pieces * unit - flat.shape[0]), (0, 0))).reshape(pieces, unit, LANES)


def from_lanes(flat, rows, width):
    flat = flat.reshape(-1, LANES)[: rows * width // LANES]
    return flat.reshape(width // LANES, rows, LANES).transpose(1, 0, 2).reshape(rows, width)


def dp_sum_direct(grad):
    rows, width = grad.shape
    members = lax.axis_size("z") * lax.axis_size("x")
    unit = -(-(rows * width // LANES) // (members * 8)) * 8
    sent = to_lanes(grad.astype(BF16), members, unit)
    got = lax.all_to_all(sent, ("z", "x"), 0, 0)
    mine = jnp.sum(got.astype(F32), axis=0)
    mine = mine + flip(mine, "yhi", 1)
    whole = broadcast_gather(mine.astype(BF16), ("z", "x"), members)
    return from_lanes(whole, rows, width).astype(F32)


def dp_sum_steps(grad):
    rows, width = grad.shape
    z, x = lax.axis_index("z"), lax.axis_index("x")
    unit = -(-(rows * width // LANES) // (4 * 64)) * 64
    half = unit // 2
    parts = to_lanes(grad, 4, unit)

    def part(k):
        return lax.dynamic_index_in_dim(parts, (x + k) % 4, 0, keepdims=False)

    far = part(2).astype(BF16)
    up = shift(far[:half], "x", 1)
    down = shift(far[half:], "x", -1)
    right, left = part(1), part(3)
    up = shift(jnp.concatenate([right[:half] + up.astype(F32), right[half:]]).astype(BF16), "x", 1)
    down = shift(jnp.concatenate([left[:half], left[half:] + down.astype(F32)]).astype(BF16), "x", -1)
    mine = part(0) + up.astype(F32) + down.astype(F32)
    for bit in (1, 2, 4):
        high = (z & bit) != 0
        low_half, high_half = jnp.split(mine, 2, axis=0)
        keep = jnp.where(high, high_half, low_half)
        send = jnp.where(high, low_half, high_half)
        mine = keep + flip(send.astype(BF16), "z", bit).astype(F32)
    mine = (mine + flip(mine, "yhi", 1)).astype(BF16)
    for bit in (4, 2, 1):
        high = (z & bit) != 0
        other = flip(mine, "z", bit)
        mine = jnp.concatenate([jnp.where(high, other, mine), jnp.where(high, mine, other)], axis=0)
    from_left = shift(mine, "x", 1)
    from_right = shift(mine, "x", -1)
    far = jnp.concatenate([shift(from_left[:half], "x", 1), shift(from_right[half:], "x", -1)])
    ring = jnp.stack([mine, from_right, far, from_left])
    whole = jnp.take(ring, (jnp.arange(4) - x) % 4, axis=0)
    return from_lanes(whole, rows, width).astype(F32)


def pair_weights(left, right, label=None):
    scores = lax.dot_general(left, right, (((1,), (1,)), ((), ())), preferred_element_type=F32)
    value = jax.nn.sigmoid(SCALE * scores + OFFSET)
    if label is not None:
        value = value - label
    return (SCALE * value).astype(BF16)


def per_device(image_feats, text_feats, image_proj, text_proj):
    rows = image_feats.shape[0]
    width = image_proj.shape[1]
    quarter = rows // 4
    plane = 16
    raw = head_rows(
        jnp.concatenate(
            [
                jnp.dot(image_feats, image_proj, preferred_element_type=F32),
                jnp.dot(text_feats, text_proj, preferred_element_type=F32),
            ],
            axis=1,
        )
    )
    image_unit, image_radius = normalize(raw[:, :width])
    text_unit, text_radius = normalize(raw[:, width:])
    images = broadcast_gather(image_unit.astype(BF16), PLANE, plane).reshape(-1, width)
    texts = ring_gather(text_unit.astype(BF16))
    other_texts = flip(texts, "core", 1)
    own_place = lax.axis_index(PLANE) * quarter
    row_id = lax.broadcasted_iota(jnp.int32, (images.shape[0], texts.shape[0]), 0)
    col_id = lax.broadcasted_iota(jnp.int32, (images.shape[0], texts.shape[0]), 1)
    label = ((row_id == col_id + own_place) & (col_id < quarter)).astype(F32)
    weights = pair_weights(images, texts, label)
    other_weights = pair_weights(images, other_texts)

    def transposed(w):
        return lax.dot_general(w, images, (((0,), (0,)), ((), ())), preferred_element_type=F32)

    sent = flip(transposed(other_weights).astype(BF16), "core", 1)
    image_part = jnp.dot(weights, texts, preferred_element_type=F32) + jnp.dot(
        other_weights, other_texts, preferred_element_type=F32
    )
    image_sent = lax.all_to_all(image_part.astype(BF16).reshape(plane, quarter, width), PLANE, 0, 0)
    text_part = (transposed(weights) + sent.astype(F32)).reshape(-1, quarter, width)
    grad_text_emb = ring_sum(text_part)
    text_grad_raw = backnorm(text_unit, text_radius, grad_text_emb)
    grad_image_emb = jnp.sum(image_sent.astype(F32), axis=0)
    image_grad_raw = backnorm(image_unit, image_radius, grad_image_emb)

    piece_text = lax.all_gather(text_grad_raw, TENSOR, axis=0, tiled=True)
    piece_image = lax.all_gather(image_grad_raw, TENSOR, axis=0, tiled=True)

    def back(piece, proj):
        return lax.dot_general(
            piece, proj, (((1,), (1,)), ((), ())), preferred_element_type=F32
        ).astype(BF16)

    def outer(feats, piece):
        return lax.dot_general(feats, piece, (((0,), (0,)), ((), ())), preferred_element_type=F32)

    grad_text_w = dp_sum_steps(outer(text_feats, piece_text))
    grad_image_w = dp_sum_direct(outer(image_feats, piece_image))
    return (
        back(piece_image, image_proj),
        back(piece_text, text_proj),
        grad_image_w,
        grad_text_w,
    )


def solution(mesh):
    fine = Mesh(mesh.devices.reshape(2, 8, 4, 2, 2), AXES)
    feats = P(("yhi", "z", "x"), TENSOR)
    proj = P(TENSOR, None)
    return jax.shard_map(
        per_device,
        mesh=fine,
        in_specs=(feats, feats, proj, proj),
        out_specs=(feats, feats, proj, proj),
        check_vma=False,
    )
```

```python
import jax
import jax.numpy as jnp
from jax import lax
from jax.sharding import Mesh, PartitionSpec as P

SCALE = 10.0
OFFSET = -4.0
EPSILON = 1e-06
F32 = jnp.float32
BF16 = jnp.bfloat16

AXES = ("yhi", "z", "x", "ylo", "core")
PLANE = ("yhi", "x", "ylo")
TENSOR = ("ylo", "core")
LANES = 128


def shift(value, axis, by):
    n = lax.axis_size(axis)
    return lax.ppermute(value, axis, [(i, (i + by) % n) for i in range(n)])


def flip(value, axis, bit):
    n = lax.axis_size(axis)
    return lax.ppermute(value, axis, [(i, i ^ bit) for i in range(n)])


def broadcast_gather(value, axes, members):
    return lax.all_to_all(jnp.broadcast_to(value[None], (members,) + value.shape), axes, 0, 0)


def normalize(raw):
    radius = jnp.sqrt(jnp.sum(raw * raw, axis=1, keepdims=True) + EPSILON)
    return (raw / radius, radius)


def backnorm(unit, radius, grad):
    return ((grad - unit * jnp.sum(unit * grad, axis=1, keepdims=True)) / radius).astype(BF16)


def head_rows(partial):
    core, ylo = lax.axis_index("core"), lax.axis_index("ylo")
    rows, width = partial.shape
    parts = partial.reshape(2, 2, rows // 4, width)
    keep = lax.dynamic_index_in_dim(parts, core, 1, keepdims=False)
    send = lax.dynamic_index_in_dim(parts, 1 - core, 1, keepdims=False)
    half = keep + flip(send.astype(BF16), "core", 1).astype(F32)
    keep = lax.dynamic_index_in_dim(half, ylo, 0, keepdims=False)
    send = lax.dynamic_index_in_dim(half, 1 - ylo, 0, keepdims=False)
    return keep + flip(send.astype(BF16), "ylo", 1).astype(F32)


def column_gather(value):
    n = lax.axis_size("z")
    return jnp.concatenate([value] + [shift(value, "z", k) for k in range(1, n)], axis=0)


def column_sum(parts):
    total = parts[0]
    for k in range(1, parts.shape[0]):
        total = total + shift(parts[k].astype(BF16), "z", -k).astype(F32)
    return total


def to_tiles(grad, pieces):
    rows, width = grad.shape
    count = rows * width // (8 * LANES)
    each = -(-count // pieces)
    tiles = grad.reshape(rows // 8, 8, width // LANES, LANES).transpose(0, 2, 1, 3)
    tiles = tiles.reshape(count, 8, LANES)
    tiles = jnp.pad(tiles, ((0, pieces * each - count), (0, 0), (0, 0)))
    return tiles.reshape(pieces, each * 8, LANES)


def from_tiles(tiles, rows, width):
    count = rows * width // (8 * LANES)
    tiles = tiles.reshape(-1, 8, LANES)[:count].reshape(rows // 8, width // LANES, 8, LANES)
    return tiles.transpose(0, 2, 1, 3).reshape(rows, width)


def dp_sum_direct(grad):
    members = lax.axis_size("z") * lax.axis_size("x")
    got = lax.all_to_all(to_tiles(grad.astype(BF16), members), ("z", "x"), 0, 0)
    mine = jnp.sum(got.astype(F32), axis=0)
    mine = mine + flip(mine, "yhi", 1)
    whole = broadcast_gather(mine.astype(BF16), ("z", "x"), members)
    return from_tiles(whole, *grad.shape).astype(F32)


def cut(value, start, size):
    return lax.dynamic_slice_in_dim(value, start, size, 0)


def dp_sum_steps(grad):
    z, x = lax.axis_index("z"), lax.axis_index("x")
    unit = grad.shape[0] // 4
    half = (unit + 8) // 16 * 8

    def part(k):
        return cut(grad, (x + k) % 4 * unit, unit)

    far = part(2).astype(BF16)
    up = shift(far[:half], "x", 1)
    down = shift(far[half:], "x", -1)
    right, left = part(1), part(3)
    up = shift(jnp.concatenate([right[:half] + up.astype(F32), right[half:]]).astype(BF16), "x", 1)
    down = shift(jnp.concatenate([left[:half], left[half:] + down.astype(F32)]).astype(BF16), "x", -1)
    mine = part(0) + up.astype(F32) + down.astype(F32)
    for bit, step in ((1, 32), (2, 16), (4, 8)):
        on = (z // bit) % 2
        keep = cut(mine, on * step, step + 8)
        send = cut(mine, (1 - on) * step, step + 8).astype(BF16)
        mine = keep + flip(send, "z", bit).astype(F32)
    mine = mine.astype(BF16)
    mine = (mine.astype(F32) + flip(mine, "yhi", 1).astype(F32)).astype(BF16)
    for bit, step in ((4, 8), (2, 16), (1, 32)):
        high = (z // bit) % 2 == 1
        other = flip(mine, "z", bit)
        low = jnp.where(high, other[:step], mine[:step])
        mine = jnp.concatenate([low, jnp.where(high, mine, other)], axis=0)
    from_left = shift(mine, "x", 1)
    from_right = shift(mine, "x", -1)
    far = jnp.concatenate([shift(from_left[:half], "x", 1), shift(from_right[half:], "x", -1)])
    whole = jnp.zeros(grad.shape, F32)
    for k, value in enumerate((mine, from_right, far, from_left)):
        whole = lax.dynamic_update_slice_in_dim(whole, value.astype(F32), (x + k) % 4 * unit, 0)
    return whole


def per_device(image_feats, text_feats, image_proj, text_proj):
    width = image_proj.shape[1]
    quarter = image_feats.shape[0] // 4
    plane = 16

    def head(feats, proj):
        raw = head_rows(jnp.dot(feats, proj, preferred_element_type=F32))
        return normalize(raw)

    image_unit, image_radius = head(image_feats, image_proj)
    text_unit, text_radius = head(text_feats, text_proj)
    images = broadcast_gather(image_unit.astype(BF16), PLANE, plane).reshape(-1, width)
    texts = column_gather(text_unit.astype(BF16))
    near = texts.shape[0]
    texts = jnp.concatenate([texts, flip(texts, "core", 1)], axis=0)
    own_place = lax.axis_index(PLANE) * quarter
    scores = lax.dot_general(images, texts, (((1,), (1,)), ((), ())), preferred_element_type=F32)
    row_id = lax.broadcasted_iota(jnp.int32, scores.shape, 0)
    col_id = lax.broadcasted_iota(jnp.int32, scores.shape, 1)
    label = ((row_id == col_id + own_place) & (col_id < quarter)).astype(F32)
    weights = (SCALE * (jax.nn.sigmoid(SCALE * scores + OFFSET) - label)).astype(BF16)

    image_part = jnp.dot(weights, texts, preferred_element_type=F32).astype(BF16)
    weights, image_part = lax.optimization_barrier((weights, image_part))
    text_part = lax.dot_general(
        weights, images, (((0,), (0,)), ((), ())), preferred_element_type=F32
    )
    image_sent = lax.all_to_all(image_part.reshape(plane, quarter, width), PLANE, 0, 0)
    sent = flip(text_part[near:].astype(BF16), "core", 1)
    text_part = (text_part[:near] + sent.astype(F32)).reshape(-1, quarter, width)
    grad_text_emb = column_sum(text_part)
    text_grad_raw = backnorm(text_unit, text_radius, grad_text_emb)
    grad_image_emb = jnp.sum(image_sent.astype(F32), axis=0)
    image_grad_raw = backnorm(image_unit, image_radius, grad_image_emb)

    pieces = lax.all_gather(
        jnp.concatenate([image_grad_raw, text_grad_raw], axis=1), TENSOR, axis=0, tiled=True
    )
    piece_image, piece_text = pieces[:, :width], pieces[:, width:]

    def back(piece, proj):
        return lax.dot_general(
            piece, proj, (((1,), (1,)), ((), ())), preferred_element_type=F32
        ).astype(BF16)

    def outer(feats, piece):
        return lax.dot_general(feats, piece, (((0,), (0,)), ((), ())), preferred_element_type=F32)

    image_w = outer(image_feats, piece_image)
    text_w = outer(text_feats, piece_text)
    share = width // LANES * 2 // 3 * LANES
    direct = dp_sum_direct(jnp.concatenate([image_w, text_w[:, share:]], axis=1))
    grad_image_w = direct[:, :width]
    grad_text_w = jnp.concatenate([dp_sum_steps(text_w[:, :share]), direct[:, width:]], axis=1)
    return (
        back(piece_image, image_proj),
        back(piece_text, text_proj),
        grad_image_w,
        grad_text_w,
    )


def solution(mesh):
    fine = Mesh(mesh.devices.reshape(2, 8, 4, 2, 2), AXES)
    feats = P(("yhi", "z", "x"), TENSOR)
    proj = P(TENSOR, None)
    return jax.shard_map(
        per_device,
        mesh=fine,
        in_specs=(feats, feats, proj, proj),
        out_specs=(feats, feats, proj, proj),
        check_vma=False,
    )
```

```python
import jax
import jax.numpy as jnp
from jax import lax
from jax.sharding import Mesh, PartitionSpec as P

SCALE = 10.0
OFFSET = -4.0
EPSILON = 1e-06
F32 = jnp.float32
BF16 = jnp.bfloat16

AXES = ("yhi", "z", "x", "ylo", "core")
PLANE = ("yhi", "x", "ylo")
TENSOR = ("ylo", "core")
LANES = 128


def shift(value, axis, by):
    n = lax.axis_size(axis)
    return lax.ppermute(value, axis, [(i, (i + by) % n) for i in range(n)])


def flip(value, axis, bit):
    n = lax.axis_size(axis)
    return lax.ppermute(value, axis, [(i, i ^ bit) for i in range(n)])


def broadcast_gather(value, axes, members):
    return lax.all_to_all(jnp.broadcast_to(value[None], (members,) + value.shape), axes, 0, 0)


def normalize(raw):
    radius = jnp.sqrt(jnp.sum(raw * raw, axis=1, keepdims=True) + EPSILON)
    return (raw / radius, radius)


def backnorm(unit, radius, grad):
    return ((grad - unit * jnp.sum(unit * grad, axis=1, keepdims=True)) / radius).astype(BF16)


def core_half(partial):
    core = lax.axis_index("core")
    rows, width = partial.shape
    parts = partial.reshape(2, 2, rows // 4, width)
    keep = lax.dynamic_index_in_dim(parts, core, 1, keepdims=False)
    send = lax.dynamic_index_in_dim(parts, 1 - core, 1, keepdims=False)
    return keep + flip(send.astype(BF16), "core", 1).astype(F32)


def quarter_rows(half):
    ylo = lax.axis_index("ylo")
    keep = lax.dynamic_index_in_dim(half, ylo, 0, keepdims=False)
    send = lax.dynamic_index_in_dim(half, 1 - ylo, 0, keepdims=False)
    return keep + flip(send.astype(BF16), "ylo", 1).astype(F32)


def column_shift(value, by):
    n = lax.axis_size("z")
    pairs = [(2 * z, (z + by) % n * 2) for z in range(n)]
    pairs += [(2 * z + 1, (z - by) % n * 2 + 1) for z in range(n)]
    return lax.ppermute(value, ("z", "core"), pairs)


def column_gather(value):
    first = lax.axis_index("core") == 0
    other = flip(value, "core", 1)
    pair = jnp.concatenate([jnp.where(first, value, other), jnp.where(first, other, value)], axis=0)
    mine = [column_shift(pair, k) for k in (1, 2, 3)] + [column_shift(value, 4)]
    mine = jnp.concatenate(mine, axis=0)
    return jnp.concatenate([pair, mine, flip(mine, "core", 1)], axis=0)


def column_sum(parts, rows):
    first = lax.axis_index("core") == 0
    own = parts[: 2 * rows].astype(F32)
    far = 9 * rows
    mine = parts[2 * rows : far].astype(F32) + flip(parts[far:], "core", 1).astype(F32)
    mine = mine.astype(BF16)
    for k in (1, 2, 3):
        own = own + column_shift(mine[2 * rows * (k - 1) : 2 * rows * k], -k).astype(F32)
    half = column_shift(mine[6 * rows :], -4).astype(F32)
    send = jnp.where(first, own[rows:], own[:rows]).astype(BF16)
    return jnp.where(first, own[:rows], own[rows:]) + half + flip(send, "core", 1).astype(F32)


def cut(value, start, size):
    return lax.dynamic_slice_in_dim(value, start, size, 0)


def dp_sum_steps(grad):
    z, x = lax.axis_index("z"), lax.axis_index("x")
    unit = grad.shape[0] // 4
    half = (unit + 8) // 16 * 8

    def part(k):
        return cut(grad, (x + k) % 4 * unit, unit)

    far = part(2).astype(BF16)
    up = shift(far[:half], "x", 1)
    down = shift(far[half:], "x", -1)
    right, left = part(1), part(3)
    up = shift(jnp.concatenate([right[:half] + up.astype(F32), right[half:]]).astype(BF16), "x", 1)
    down = shift(jnp.concatenate([left[:half], left[half:] + down.astype(F32)]).astype(BF16), "x", -1)
    mine = part(0) + up.astype(F32) + down.astype(F32)
    for bit, step in ((1, 32), (2, 16), (4, 8)):
        on = (z // bit) % 2
        keep = cut(mine, on * step, step + 8)
        send = cut(mine, (1 - on) * step, step + 8).astype(BF16)
        mine = keep + flip(send, "z", bit).astype(F32)
    mine = mine.astype(BF16)
    mine = (mine.astype(F32) + flip(mine, "yhi", 1).astype(F32)).astype(BF16)
    for bit, step in ((4, 8), (2, 16), (1, 32)):
        high = (z // bit) % 2 == 1
        other = flip(mine, "z", bit)
        low = jnp.where(high, other[:step], mine[:step])
        mine = jnp.concatenate([low, jnp.where(high, mine, other)], axis=0)
    from_left = shift(mine, "x", 1)
    from_right = shift(mine, "x", -1)
    far = jnp.concatenate([shift(from_left[:half], "x", 1), shift(from_right[half:], "x", -1)])
    whole = jnp.zeros(grad.shape, F32)
    for k, value in enumerate((mine, from_right, far, from_left)):
        whole = lax.dynamic_update_slice_in_dim(whole, value.astype(F32), (x + k) % 4 * unit, 0)
    return whole


def dp_sum_column(grad):
    z, n = lax.axis_index("z"), lax.axis_size("z")
    unit = grad.shape[0] // n

    def block(k):
        return cut(grad, (z + n + k) % n * unit, unit)

    down = shift(block(-4).astype(BF16), "z", -1)
    up = shift(block(3).astype(BF16), "z", 1)
    for step in (3, 2, 1):
        down = shift((block(-step) + down.astype(F32)).astype(BF16), "z", -1)
        if step > 1:
            up = shift((block(step - 1) + up.astype(F32)).astype(BF16), "z", 1)
    mine = block(0) + down.astype(F32) + up.astype(F32)
    for axis, bit in (("x", 1), ("x", 2), ("yhi", 1)):
        sent = mine.astype(BF16)
        mine = sent.astype(F32) + flip(sent, axis, bit).astype(F32)
    up = down = mine.astype(BF16)
    got = [(0, up)]
    for step in range(1, 5):
        up = shift(up, "z", 1)
        got.append((-step, up))
        if step < 4:
            down = shift(down, "z", -1)
            got.append((step, down))
    whole = jnp.zeros(grad.shape, F32)
    for k, value in got:
        whole = lax.dynamic_update_slice_in_dim(whole, value.astype(F32), (z + n + k) % n * unit, 0)
    return whole


def per_device(image_feats, text_feats, image_proj, text_proj):
    width = image_proj.shape[1]
    quarter = image_feats.shape[0] // 4
    plane = 16

    image_half = core_half(jnp.dot(image_feats, image_proj, preferred_element_type=F32))
    text_half = core_half(jnp.dot(text_feats, text_proj, preferred_element_type=F32))
    image_unit, image_radius = normalize(quarter_rows(image_half))
    text_half, image_unit = lax.optimization_barrier((text_half, image_unit))
    text_unit, text_radius = normalize(quarter_rows(text_half))
    images = broadcast_gather(image_unit.astype(BF16), PLANE, plane).reshape(-1, width)
    texts = column_gather(text_unit.astype(BF16))
    own_image = lax.axis_index(PLANE) * quarter
    own_text = lax.axis_index("core") * quarter
    scores = lax.dot_general(images, texts, (((1,), (1,)), ((), ())), preferred_element_type=F32)
    row_id = lax.broadcasted_iota(jnp.int32, scores.shape, 0)
    col_id = lax.broadcasted_iota(jnp.int32, scores.shape, 1)
    label = (row_id - own_image == col_id - own_text) & (col_id // quarter == own_text // quarter)
    weights = (SCALE * (jax.nn.sigmoid(SCALE * scores + OFFSET) - label.astype(F32))).astype(BF16)

    image_part = jnp.dot(weights, texts, preferred_element_type=F32).astype(BF16)
    weights, image_part = lax.optimization_barrier((weights, image_part))
    text_part = lax.dot_general(
        weights, images, (((0,), (0,)), ((), ())), preferred_element_type=F32
    )
    image_sent = lax.all_to_all(image_part.reshape(plane, quarter, width), PLANE, 0, 0)
    grad_text_emb = column_sum(text_part.astype(BF16), quarter)
    text_grad_raw = backnorm(text_unit, text_radius, grad_text_emb)
    grad_image_emb = jnp.sum(image_sent.astype(F32), axis=0)
    image_grad_raw = backnorm(image_unit, image_radius, grad_image_emb)

    pieces = lax.all_gather(
        jnp.concatenate([image_grad_raw, text_grad_raw], axis=1), TENSOR, axis=0, tiled=True
    )
    piece_image, piece_text = pieces[:, :width], pieces[:, width:]

    def back(piece, proj):
        return lax.dot_general(
            piece, proj, (((1,), (1,)), ((), ())), preferred_element_type=F32
        ).astype(BF16)

    def outer(feats, piece):
        return lax.dot_general(feats, piece, (((0,), (0,)), ((), ())), preferred_element_type=F32)

    slice_rows = text_feats.shape[1]
    padded = jnp.pad(text_feats, ((0, 0), (0, -slice_rows % 64)))
    grad_text_w = dp_sum_column(outer(padded, piece_text))[:slice_rows]
    grad_image_w = dp_sum_steps(outer(image_feats, piece_image))
    return (
        back(piece_image, image_proj),
        back(piece_text, text_proj),
        grad_image_w,
        grad_text_w,
    )


def solution(mesh):
    fine = Mesh(mesh.devices.reshape(2, 8, 4, 2, 2), AXES)
    feats = P(("yhi", "z", "x"), TENSOR)
    proj = P(TENSOR, None)
    return jax.shard_map(
        per_device,
        mesh=fine,
        in_specs=(feats, feats, proj, proj),
        out_specs=(feats, feats, proj, proj),
        check_vma=False,
    )
```

```python
import jax
import jax.numpy as jnp
from jax import lax
from jax.sharding import Mesh, PartitionSpec as P

SCALE = 10.0
OFFSET = -4.0
EPSILON = 1e-06
F32 = jnp.float32
BF16 = jnp.bfloat16

AXES = ("yhi", "z", "x", "ylo", "core")
PLANE = ("yhi", "x", "ylo")
TENSOR = ("ylo", "core")
LANES = 128


def shift(value, axis, by):
    n = lax.axis_size(axis)
    return lax.ppermute(value, axis, [(i, (i + by) % n) for i in range(n)])


def flip(value, axis, bit):
    n = lax.axis_size(axis)
    return lax.ppermute(value, axis, [(i, i ^ bit) for i in range(n)])


def broadcast_gather(value, axes, members):
    return lax.all_to_all(jnp.broadcast_to(value[None], (members,) + value.shape), axes, 0, 0)


def normalize(raw):
    radius = jnp.sqrt(jnp.sum(raw * raw, axis=1, keepdims=True) + EPSILON)
    return (raw / radius, radius)


def backnorm(unit, radius, grad):
    return ((grad - unit * jnp.sum(unit * grad, axis=1, keepdims=True)) / radius).astype(BF16)


def core_half(partial):
    core = lax.axis_index("core")
    rows, width = partial.shape
    parts = partial.reshape(2, 2, rows // 4, width)
    keep = lax.dynamic_index_in_dim(parts, core, 1, keepdims=False)
    send = lax.dynamic_index_in_dim(parts, 1 - core, 1, keepdims=False)
    return keep + flip(send.astype(BF16), "core", 1).astype(F32)


def quarter_rows(half):
    ylo = lax.axis_index("ylo")
    keep = lax.dynamic_index_in_dim(half, ylo, 0, keepdims=False)
    send = lax.dynamic_index_in_dim(half, 1 - ylo, 0, keepdims=False)
    return keep + flip(send.astype(BF16), "ylo", 1).astype(F32)


def column_shift(value, by):
    n = lax.axis_size("z")
    pairs = [(2 * z, (z + by) % n * 2) for z in range(n)]
    pairs += [(2 * z + 1, (z - by) % n * 2 + 1) for z in range(n)]
    return lax.ppermute(value, ("z", "core"), pairs)


def column_gather(value):
    first = lax.axis_index("core") == 0
    other = flip(value, "core", 1)
    pair = jnp.concatenate([jnp.where(first, value, other), jnp.where(first, other, value)], axis=0)
    far = column_shift(value, 4)
    got = {k: column_shift(pair, k) for k in (3, 2, 1)}
    mine = jnp.concatenate([got[1], got[2], got[3], far], axis=0)
    return jnp.concatenate([pair, mine, flip(mine, "core", 1)], axis=0)


def column_sum(parts, rows):
    first = lax.axis_index("core") == 0
    own = parts[: 2 * rows].astype(F32)
    far = 9 * rows
    mine = parts[2 * rows : far].astype(F32) + flip(parts[far:], "core", 1).astype(F32)
    mine = mine.astype(BF16)
    half = column_shift(mine[6 * rows :], -4).astype(F32)
    for k in (3, 2, 1):
        own = own + column_shift(mine[2 * rows * (k - 1) : 2 * rows * k], -k).astype(F32)
    send = jnp.where(first, own[rows:], own[:rows]).astype(BF16)
    return jnp.where(first, own[:rows], own[rows:]) + half + flip(send, "core", 1).astype(F32)


def to_tiles(grad, pieces):
    rows, width = grad.shape
    count = rows * width // (8 * LANES)
    each = -(-count // pieces)
    tiles = grad.reshape(rows // 8, 8, width // LANES, LANES).transpose(0, 2, 1, 3)
    tiles = tiles.reshape(count, 8, LANES)
    tiles = jnp.pad(tiles, ((0, pieces * each - count), (0, 0), (0, 0)))
    return tiles.reshape(pieces, each * 8, LANES)


def from_tiles(tiles, rows, width):
    count = rows * width // (8 * LANES)
    tiles = tiles.reshape(-1, 8, LANES)[:count].reshape(rows // 8, width // LANES, 8, LANES)
    return tiles.transpose(0, 2, 1, 3).reshape(rows, width)


def column_scatter_sum(tiles):
    z, n = lax.axis_index("z"), lax.axis_size("z")
    sign = 1 - 2 * lax.axis_index("core")

    def block(k):
        return lax.dynamic_index_in_dim(tiles, (z + n + k) % n, 0, keepdims=False)

    away = jnp.stack([block(-sign * k) for k in (1, 2, 3)]).astype(BF16)
    got = flip(away, "core", 1)
    mine = block(0) + column_shift(block(4).astype(BF16), 4).astype(F32)
    pairs = {
        k: column_shift(jnp.stack([block(sign * k).astype(BF16), got[k - 1]]), k) for k in (3, 2, 1)
    }
    theirs = sum(pairs[k][1].astype(F32) for k in (1, 2, 3)).astype(BF16)
    mine = mine + sum(pairs[k][0].astype(F32) for k in (1, 2, 3))
    return mine + flip(theirs, "core", 1).astype(F32)


def column_spread(value):
    z, n = lax.axis_index("z"), lax.axis_size("z")
    first = lax.axis_index("core") == 0
    pair = jnp.stack([value, flip(value, "core", 1)])
    far = column_shift(value, 4)
    got = {k: column_shift(pair, k) for k in (3, 2, 1)}
    far, got = lax.optimization_barrier((far, got))
    swapped = flip(jnp.stack([got[k][1] for k in (1, 2, 3)]), "core", 1)
    above = [jnp.where(first, swapped[k - 1], got[k][0]) for k in (1, 2, 3)]
    below = [jnp.where(first, got[k][0], swapped[k - 1]) for k in (3, 2, 1)]
    ring = [value] + above + [far] + below
    return lax.dynamic_slice_in_dim(jnp.stack(ring + ring), (n - z) % n, n, 0)


def dp_sum(grads):
    x = lax.axis_index("x")
    rows, width = grads[0].shape
    unit = rows // 4
    half = (unit + 8) // 16 * 8

    def part(k):
        start = (x + k) % 4 * unit
        return jnp.stack([lax.dynamic_slice_in_dim(g, start, unit, 0) for g in grads])

    far = part(2).astype(BF16)
    up = shift(far[:, :half], "x", 1)
    down = shift(far[:, half:], "x", -1)
    right, left = part(1), part(3)
    up = jnp.concatenate([right[:, :half] + up.astype(F32), right[:, half:]], axis=1)
    down = jnp.concatenate([left[:, :half], left[:, half:] + down.astype(F32)], axis=1)
    up = shift(up.astype(BF16), "x", 1)
    down = shift(down.astype(BF16), "x", -1)
    mine = part(0) + up.astype(F32) + down.astype(F32)
    tiles = to_tiles(mine.reshape(2 * unit, width), lax.axis_size("z"))
    sent = column_scatter_sum(tiles).astype(BF16)
    total = (sent.astype(F32) + flip(sent, "yhi", 1).astype(F32)).astype(BF16)
    mine = from_tiles(column_spread(total), 2 * unit, width).reshape(2, unit, width)
    from_left = shift(mine, "x", 1)
    from_right = shift(mine, "x", -1)
    up = shift(from_left[:, :half], "x", 1)
    down = shift(from_right[:, half:], "x", -1)
    out = []
    for h in range(2):
        whole = jnp.zeros((rows, width), F32)
        far = jnp.concatenate([up[h], down[h]], axis=0)
        for k, value in enumerate((mine[h], from_right[h], far, from_left[h])):
            place = (x + k) % 4 * unit
            whole = lax.dynamic_update_slice_in_dim(whole, value.astype(F32), place, 0)
        out.append(whole)
    return out


def per_device(image_feats, text_feats, image_proj, text_proj):
    width = image_proj.shape[1]
    quarter = image_feats.shape[0] // 4
    plane = 16

    image_half = core_half(jnp.dot(image_feats, image_proj, preferred_element_type=F32))
    text_half = core_half(jnp.dot(text_feats, text_proj, preferred_element_type=F32))
    image_unit, image_radius = normalize(quarter_rows(image_half))
    text_half, image_unit = lax.optimization_barrier((text_half, image_unit))
    text_unit, text_radius = normalize(quarter_rows(text_half))
    images = broadcast_gather(image_unit.astype(BF16), PLANE, plane).reshape(-1, width)
    texts = column_gather(text_unit.astype(BF16))
    own_image = lax.axis_index(PLANE) * quarter
    own_text = lax.axis_index("core") * quarter
    scores = lax.dot_general(images, texts, (((1,), (1,)), ((), ())), preferred_element_type=F32)
    row_id = lax.broadcasted_iota(jnp.int32, scores.shape, 0)
    col_id = lax.broadcasted_iota(jnp.int32, scores.shape, 1)
    label = (row_id - own_image == col_id - own_text) & (col_id // quarter == own_text // quarter)
    weights = (SCALE * (jax.nn.sigmoid(SCALE * scores + OFFSET) - label.astype(F32))).astype(BF16)

    image_part = jnp.dot(weights, texts, preferred_element_type=F32).astype(BF16)
    weights, image_part = lax.optimization_barrier((weights, image_part))
    text_part = lax.dot_general(
        weights, images, (((0,), (0,)), ((), ())), preferred_element_type=F32
    )
    image_sent = lax.all_to_all(image_part.reshape(plane, quarter, width), PLANE, 0, 0)
    grad_text_emb = column_sum(text_part.astype(BF16), quarter)
    text_grad_raw = backnorm(text_unit, text_radius, grad_text_emb)
    grad_image_emb = jnp.sum(image_sent.astype(F32), axis=0)
    image_grad_raw = backnorm(image_unit, image_radius, grad_image_emb)

    pieces = lax.all_gather(
        jnp.concatenate([image_grad_raw, text_grad_raw], axis=1), TENSOR, axis=0, tiled=True
    )
    piece_image, piece_text = pieces[:, :width], pieces[:, width:]

    def back(piece, proj):
        return lax.dot_general(
            piece, proj, (((1,), (1,)), ((), ())), preferred_element_type=F32
        ).astype(BF16)

    def outer(feats, piece):
        return lax.dot_general(feats, piece, (((0,), (0,)), ((), ())), preferred_element_type=F32)

    grad_image_w, grad_text_w = dp_sum(
        [outer(image_feats, piece_image), outer(text_feats, piece_text)]
    )
    return (
        back(piece_image, image_proj),
        back(piece_text, text_proj),
        grad_image_w,
        grad_text_w,
    )


def solution(mesh):
    fine = Mesh(mesh.devices.reshape(2, 8, 4, 2, 2), AXES)
    feats = P(("yhi", "z", "x"), TENSOR)
    proj = P(TENSOR, None)
    return jax.shard_map(
        per_device,
        mesh=fine,
        in_specs=(feats, feats, proj, proj),
        out_specs=(feats, feats, proj, proj),
        check_vma=False,
    )
```

```python
import jax
import jax.numpy as jnp
from jax import lax
from jax.sharding import Mesh, PartitionSpec as P

SCALE = 10.0
OFFSET = -4.0
EPSILON = 1e-06
F32 = jnp.float32
BF16 = jnp.bfloat16

AXES = ("yhi", "z", "x", "ylo", "core")
PLANE = ("yhi", "x", "ylo")
TENSOR = ("ylo", "core")
LANES = 128


def shift(value, axis, by):
    n = lax.axis_size(axis)
    return lax.ppermute(value, axis, [(i, (i + by) % n) for i in range(n)])


def flip(value, axis, bit):
    n = lax.axis_size(axis)
    return lax.ppermute(value, axis, [(i, i ^ bit) for i in range(n)])


def normalize(raw):
    radius = jnp.sqrt(jnp.sum(raw * raw, axis=1, keepdims=True) + EPSILON)
    return (raw / radius, radius)


def backnorm(unit, radius, grad):
    return ((grad - unit * jnp.sum(unit * grad, axis=1, keepdims=True)) / radius).astype(BF16)


def core_half(partial):
    core = lax.axis_index("core")
    rows, width = partial.shape
    parts = partial.reshape(2, 2, rows // 4, width)
    keep = lax.dynamic_index_in_dim(parts, core, 1, keepdims=False)
    send = lax.dynamic_index_in_dim(parts, 1 - core, 1, keepdims=False)
    return keep + flip(send.astype(BF16), "core", 1).astype(F32)


def quarter_rows(half):
    ylo = lax.axis_index("ylo")
    keep = lax.dynamic_index_in_dim(half, ylo, 0, keepdims=False)
    send = lax.dynamic_index_in_dim(half, 1 - ylo, 0, keepdims=False)
    return keep + flip(send.astype(BF16), "ylo", 1).astype(F32)


def column_shift(value, by):
    n = lax.axis_size("z")
    pairs = [(2 * z, (z + by) % n * 2) for z in range(n)]
    pairs += [(2 * z + 1, (z - by) % n * 2 + 1) for z in range(n)]
    return lax.ppermute(value, ("z", "core"), pairs)


def column_gather(value):
    first = lax.axis_index("core") == 0
    other = flip(value, "core", 1)
    pair = jnp.concatenate([jnp.where(first, value, other), jnp.where(first, other, value)], axis=0)
    far = column_shift(value, 4)
    got = {k: column_shift(pair, k) for k in (3, 2, 1)}
    mine = jnp.concatenate([got[1], got[2], got[3], far], axis=0)
    return jnp.concatenate([pair, mine, flip(mine, "core", 1)], axis=0)


def column_sum(parts, swapped, rows):
    first = lax.axis_index("core") == 0
    own = parts[: 2 * rows].astype(F32)

    def sent(start, stop):
        mine = parts[2 * rows + start : 2 * rows + stop].astype(F32)
        return (mine + swapped[start:stop].astype(F32)).astype(BF16)

    half = column_shift(sent(6 * rows, 7 * rows), -4).astype(F32)
    for k in (3, 2, 1):
        own = own + column_shift(sent(2 * rows * (k - 1), 2 * rows * k), -k).astype(F32)
    send = jnp.where(first, own[rows:], own[:rows]).astype(BF16)
    return jnp.where(first, own[:rows], own[rows:]) + half + flip(send, "core", 1).astype(F32)


def to_tiles(grad, pieces):
    rows, width = grad.shape
    count = rows * width // (8 * LANES)
    each = -(-count // pieces)
    tiles = grad.reshape(rows // 8, 8, width // LANES, LANES).transpose(0, 2, 1, 3)
    tiles = tiles.reshape(count, 8, LANES)
    tiles = jnp.pad(tiles, ((0, pieces * each - count), (0, 0), (0, 0)))
    return tiles.reshape(pieces, each * 8, LANES)


def from_tiles(tiles, rows, width):
    count = rows * width // (8 * LANES)
    tiles = tiles.reshape(-1, 8, LANES)[:count].reshape(rows // 8, width // LANES, 8, LANES)
    return tiles.transpose(0, 2, 1, 3).reshape(rows, width)


def column_scatter_sum(tiles):
    z, n = lax.axis_index("z"), lax.axis_size("z")
    sign = 1 - 2 * lax.axis_index("core")

    def block(k):
        return lax.dynamic_index_in_dim(tiles, (z + n + k) % n, 0, keepdims=False)

    away = jnp.stack([block(-sign * k) for k in (1, 2, 3)]).astype(BF16)
    got = flip(away, "core", 1)
    mine = block(0) + column_shift(block(4).astype(BF16), 4).astype(F32)
    pairs = {
        k: column_shift(jnp.stack([block(sign * k).astype(BF16), got[k - 1]]), k) for k in (3, 2, 1)
    }
    theirs = sum(pairs[k][1].astype(F32) for k in (1, 2, 3)).astype(BF16)
    mine = mine + sum(pairs[k][0].astype(F32) for k in (1, 2, 3))
    return mine + flip(theirs, "core", 1).astype(F32)


def column_spread(value):
    z, n = lax.axis_index("z"), lax.axis_size("z")
    first = lax.axis_index("core") == 0
    pair = jnp.stack([value, flip(value, "core", 1)])
    far = column_shift(value, 4)
    got = {k: column_shift(pair, k) for k in (3, 2, 1)}
    far, got = lax.optimization_barrier((far, got))
    swapped = flip(jnp.stack([got[k][1] for k in (1, 2, 3)]), "core", 1)
    above = [jnp.where(first, swapped[k - 1], got[k][0]) for k in (1, 2, 3)]
    below = [jnp.where(first, got[k][0], swapped[k - 1]) for k in (3, 2, 1)]
    ring = [value] + above + [far] + below
    return lax.dynamic_slice_in_dim(jnp.stack(ring + ring), (n - z) % n, n, 0)


def dp_sum(grads):
    x = lax.axis_index("x")
    rows, width = grads[0].shape
    unit = rows // 4
    half = (unit + 8) // 16 * 8

    def part(k):
        start = (x + k) % 4 * unit
        return jnp.stack([lax.dynamic_slice_in_dim(g, start, unit, 0) for g in grads])

    far = part(2).astype(BF16)
    up = shift(far[:, :half], "x", 1)
    down = shift(far[:, half:], "x", -1)
    right, left = part(1), part(3)
    up = jnp.concatenate([right[:, :half] + up.astype(F32), right[:, half:]], axis=1)
    down = jnp.concatenate([left[:, :half], left[:, half:] + down.astype(F32)], axis=1)
    up = shift(up.astype(BF16), "x", 1)
    down = shift(down.astype(BF16), "x", -1)
    mine = part(0) + up.astype(F32) + down.astype(F32)
    tiles = to_tiles(mine.reshape(2 * unit, width), lax.axis_size("z"))
    sent = column_scatter_sum(tiles).astype(BF16)
    total = (sent.astype(F32) + flip(sent, "yhi", 1).astype(F32)).astype(BF16)
    mine = from_tiles(column_spread(total), 2 * unit, width).reshape(2, unit, width)
    from_left = shift(mine, "x", 1)
    from_right = shift(mine, "x", -1)
    up = shift(from_left[:, :half], "x", 1)
    down = shift(from_right[:, half:], "x", -1)
    out = []
    for h in range(2):
        whole = jnp.zeros((rows, width), F32)
        far = jnp.concatenate([up[h], down[h]], axis=0)
        for k, value in enumerate((mine[h], from_right[h], far, from_left[h])):
            place = (x + k) % 4 * unit
            whole = lax.dynamic_update_slice_in_dim(whole, value.astype(F32), place, 0)
        out.append(whole)
    return out


def per_device(image_feats, text_feats, image_proj, text_proj):
    width = image_proj.shape[1]
    quarter = image_feats.shape[0] // 4
    plane = 16

    image_half = core_half(jnp.dot(image_feats, image_proj, preferred_element_type=F32))
    text_half = core_half(jnp.dot(text_feats, text_proj, preferred_element_type=F32))
    image_unit, image_radius = normalize(quarter_rows(image_half))
    text_unit, text_radius = normalize(quarter_rows(text_half))
    spread = jnp.broadcast_to(image_unit.astype(BF16)[None], (plane, quarter, width))
    spread, text_emb = lax.optimization_barrier((spread, text_unit.astype(BF16)))
    images = lax.all_to_all(spread, PLANE, 0, 0).reshape(-1, width)
    texts = column_gather(text_emb)
    own_image = lax.axis_index(PLANE) * quarter
    own_text = lax.axis_index("core") * quarter
    scores = lax.dot_general(images, texts, (((1,), (1,)), ((), ())), preferred_element_type=F32)
    row_id = lax.broadcasted_iota(jnp.int32, scores.shape, 0)
    col_id = lax.broadcasted_iota(jnp.int32, scores.shape, 1)
    label = (row_id - own_image == col_id - own_text) & (col_id // quarter == own_text // quarter)
    weights = (SCALE * (jax.nn.sigmoid(SCALE * scores + OFFSET) - label.astype(F32))).astype(BF16)

    text_part = lax.dot_general(
        weights, images, (((0,), (0,)), ((), ())), preferred_element_type=F32
    ).astype(BF16)
    swapped = flip(text_part[9 * quarter :], "core", 1)
    weights, text_part = lax.optimization_barrier((weights, text_part))
    image_part = jnp.dot(weights, texts, preferred_element_type=F32).astype(BF16)
    image_part, swapped = lax.optimization_barrier((image_part, swapped))
    image_sent = lax.all_to_all(image_part.reshape(plane, quarter, width), PLANE, 0, 0)
    grad_text_emb = column_sum(text_part, swapped, quarter)
    text_grad_raw = backnorm(text_unit, text_radius, grad_text_emb)
    grad_image_emb = jnp.sum(image_sent.astype(F32), axis=0)
    image_grad_raw = backnorm(image_unit, image_radius, grad_image_emb)

    pieces = lax.all_gather(
        jnp.concatenate([image_grad_raw, text_grad_raw], axis=1), TENSOR, axis=0, tiled=True
    )
    piece_image, piece_text = pieces[:, :width], pieces[:, width:]

    def back(piece, proj):
        return lax.dot_general(
            piece, proj, (((1,), (1,)), ((), ())), preferred_element_type=F32
        ).astype(BF16)

    def outer(feats, piece):
        return lax.dot_general(feats, piece, (((0,), (0,)), ((), ())), preferred_element_type=F32)

    grad_image_w, grad_text_w = dp_sum(
        [outer(image_feats, piece_image), outer(text_feats, piece_text)]
    )
    return (
        back(piece_image, image_proj),
        back(piece_text, text_proj),
        grad_image_w,
        grad_text_w,
    )


def solution(mesh):
    fine = Mesh(mesh.devices.reshape(2, 8, 4, 2, 2), AXES)
    feats = P(("yhi", "z", "x"), TENSOR)
    proj = P(TENSOR, None)
    return jax.shard_map(
        per_device,
        mesh=fine,
        in_specs=(feats, feats, proj, proj),
        out_specs=(feats, feats, proj, proj),
        check_vma=False,
    )
```

```python
import jax
import jax.numpy as jnp
from jax import lax
from jax.sharding import Mesh, PartitionSpec as P

SCALE = 10.0
OFFSET = -4.0
EPSILON = 1e-06
F32 = jnp.float32
BF16 = jnp.bfloat16

AXES = ("yhi", "z", "x", "ylo", "core")
PLANE = ("yhi", "x", "ylo")
TENSOR = ("ylo", "core")
LANES = 128


def shift(value, axis, by):
    n = lax.axis_size(axis)
    return lax.ppermute(value, axis, [(i, (i + by) % n) for i in range(n)])


def flip(value, axis, bit):
    n = lax.axis_size(axis)
    return lax.ppermute(value, axis, [(i, i ^ bit) for i in range(n)])


def normalize(raw):
    radius = jnp.sqrt(jnp.sum(raw * raw, axis=1, keepdims=True) + EPSILON)
    return (raw / radius, radius)


def backnorm(unit, radius, grad):
    return ((grad - unit * jnp.sum(unit * grad, axis=1, keepdims=True)) / radius).astype(BF16)


def core_half(partial):
    core = lax.axis_index("core")
    rows, width = partial.shape
    parts = partial.reshape(2, 2, rows // 4, width)
    keep = lax.dynamic_index_in_dim(parts, core, 1, keepdims=False)
    send = lax.dynamic_index_in_dim(parts, 1 - core, 1, keepdims=False)
    return keep + flip(send.astype(BF16), "core", 1).astype(F32)


def quarter_rows(half):
    ylo = lax.axis_index("ylo")
    keep = lax.dynamic_index_in_dim(half, ylo, 0, keepdims=False)
    send = lax.dynamic_index_in_dim(half, 1 - ylo, 0, keepdims=False)
    return keep + flip(send.astype(BF16), "ylo", 1).astype(F32)


def column_shift(value, by):
    n = lax.axis_size("z")
    pairs = [(2 * z, (z + by) % n * 2) for z in range(n)]
    pairs += [(2 * z + 1, (z - by) % n * 2 + 1) for z in range(n)]
    return lax.ppermute(value, ("z", "core"), pairs)


def column_gather(value):
    first = lax.axis_index("core") == 0
    other = flip(value, "core", 1)
    pair = jnp.concatenate([jnp.where(first, value, other), jnp.where(first, other, value)], axis=0)
    far = column_shift(value, 4)
    got = {k: column_shift(pair, k) for k in (3, 2, 1)}
    mine = lax.optimization_barrier(jnp.concatenate([got[1], got[2], got[3], far], axis=0))
    return jnp.concatenate([pair, mine, flip(mine, "core", 1)], axis=0)


def column_sum(parts, swapped, rows):
    first = lax.axis_index("core") == 0
    own = parts[: 2 * rows].astype(F32)

    def sent(start, stop):
        mine = parts[2 * rows + start : 2 * rows + stop].astype(F32)
        return (mine + swapped[start:stop].astype(F32)).astype(BF16)

    half = column_shift(sent(6 * rows, 7 * rows), -4).astype(F32)
    for k in (3, 2, 1):
        own = own + column_shift(sent(2 * rows * (k - 1), 2 * rows * k), -k).astype(F32)
    send = jnp.where(first, own[rows:], own[:rows]).astype(BF16)
    return jnp.where(first, own[:rows], own[rows:]) + half + flip(send, "core", 1).astype(F32)


def to_tiles(grad, pieces):
    rows, width = grad.shape
    count = rows * width // (8 * LANES)
    each = -(-count // pieces)
    tiles = grad.reshape(rows // 8, 8, width // LANES, LANES).transpose(0, 2, 1, 3)
    tiles = tiles.reshape(count, 8, LANES)
    tiles = jnp.pad(tiles, ((0, pieces * each - count), (0, 0), (0, 0)))
    return tiles.reshape(pieces, each * 8, LANES)


def from_tiles(tiles, rows, width):
    count = rows * width // (8 * LANES)
    tiles = tiles.reshape(-1, 8, LANES)[:count].reshape(rows // 8, width // LANES, 8, LANES)
    return tiles.transpose(0, 2, 1, 3).reshape(rows, width)


def column_scatter_sum(tiles):
    z, n = lax.axis_index("z"), lax.axis_size("z")
    sign = 1 - 2 * lax.axis_index("core")

    def block(k):
        return lax.dynamic_index_in_dim(tiles, (z + n + k) % n, 0, keepdims=False)

    away = jnp.stack([block(-sign * k) for k in (1, 2, 3)]).astype(BF16)
    got = flip(away, "core", 1)
    mine = block(0) + column_shift(block(4).astype(BF16), 4).astype(F32)
    pairs = {
        k: column_shift(jnp.stack([block(sign * k).astype(BF16), got[k - 1]]), k) for k in (3, 2, 1)
    }
    theirs = sum(pairs[k][1].astype(F32) for k in (1, 2, 3)).astype(BF16)
    mine = mine + sum(pairs[k][0].astype(F32) for k in (1, 2, 3))
    return mine + flip(theirs, "core", 1).astype(F32)


def column_spread(value):
    z, n = lax.axis_index("z"), lax.axis_size("z")
    first = lax.axis_index("core") == 0
    pair = jnp.stack([value, flip(value, "core", 1)])
    far = column_shift(value, 4)
    got = {k: column_shift(pair, k) for k in (3, 2, 1)}
    far, got = lax.optimization_barrier((far, got))
    swapped = flip(jnp.stack([got[k][1] for k in (1, 2, 3)]), "core", 1)
    above = [jnp.where(first, swapped[k - 1], got[k][0]) for k in (1, 2, 3)]
    below = [jnp.where(first, got[k][0], swapped[k - 1]) for k in (3, 2, 1)]
    ring = [value] + above + [far] + below
    return lax.dynamic_slice_in_dim(jnp.stack(ring + ring), (n - z) % n, n, 0)


def dp_sum(grads):
    x = lax.axis_index("x")
    rows, width = grads[0].shape
    unit = rows // 4
    half = (unit + 8) // 16 * 8

    def part(k):
        start = (x + k) % 4 * unit
        return jnp.stack([lax.dynamic_slice_in_dim(g, start, unit, 0) for g in grads])

    far = part(2).astype(BF16)
    up = shift(far[:, :half], "x", 1)
    down = shift(far[:, half:], "x", -1)
    right, left = part(1), part(3)
    up = jnp.concatenate([right[:, :half] + up.astype(F32), right[:, half:]], axis=1)
    down = jnp.concatenate([left[:, :half], left[:, half:] + down.astype(F32)], axis=1)
    up = shift(up.astype(BF16), "x", 1)
    down = shift(down.astype(BF16), "x", -1)
    mine = part(0) + up.astype(F32) + down.astype(F32)
    tiles = to_tiles(mine.reshape(2 * unit, width), lax.axis_size("z"))
    sent = column_scatter_sum(tiles).astype(BF16)
    total = (sent.astype(F32) + flip(sent, "yhi", 1).astype(F32)).astype(BF16)
    mine = from_tiles(column_spread(total), 2 * unit, width).reshape(2, unit, width)
    from_left = shift(mine, "x", 1)
    from_right = shift(mine, "x", -1)
    up = shift(from_left[:, :half], "x", 1)
    down = shift(from_right[:, half:], "x", -1)
    out = []
    for h in range(2):
        whole = jnp.zeros((rows, width), F32)
        far = jnp.concatenate([up[h], down[h]], axis=0)
        for k, value in enumerate((mine[h], from_right[h], far, from_left[h])):
            place = (x + k) % 4 * unit
            whole = lax.dynamic_update_slice_in_dim(whole, value.astype(F32), place, 0)
        out.append(whole)
    return out


def per_device(image_feats, text_feats, image_proj, text_proj):
    width = image_proj.shape[1]
    quarter = image_feats.shape[0] // 4
    plane = 16

    image_half = core_half(jnp.dot(image_feats, image_proj, preferred_element_type=F32))
    text_half = core_half(jnp.dot(text_feats, text_proj, preferred_element_type=F32))
    image_unit, image_radius = normalize(quarter_rows(image_half))
    text_unit, text_radius = normalize(quarter_rows(text_half))
    spread = jnp.broadcast_to(image_unit.astype(BF16)[None], (plane, quarter, width))
    spread, text_emb = lax.optimization_barrier((spread, text_unit.astype(BF16)))
    images = lax.all_to_all(spread, PLANE, 0, 0).reshape(-1, width)
    texts = column_gather(text_emb)
    own_image = lax.axis_index(PLANE) * quarter
    own_text = lax.axis_index("core") * quarter
    scores = lax.dot_general(images, texts, (((1,), (1,)), ((), ())), preferred_element_type=F32)
    row_id = lax.broadcasted_iota(jnp.int32, scores.shape, 0)
    col_id = lax.broadcasted_iota(jnp.int32, scores.shape, 1)
    own_id = col_id - own_text
    label = (row_id == own_id + own_image) & (own_id >= 0) & (own_id < quarter)
    weights = (SCALE * (jax.nn.sigmoid(SCALE * scores + OFFSET) - label.astype(F32))).astype(BF16)

    text_part = lax.dot_general(
        weights, images, (((0,), (0,)), ((), ())), preferred_element_type=F32
    ).astype(BF16)
    swapped = flip(text_part[9 * quarter :], "core", 1)
    weights, text_part = lax.optimization_barrier((weights, text_part))
    image_part = jnp.dot(weights, texts, preferred_element_type=F32).astype(BF16)
    image_part, swapped = lax.optimization_barrier((image_part, swapped))
    image_sent = lax.all_to_all(image_part.reshape(plane, quarter, width), PLANE, 0, 0)
    grad_text_emb = column_sum(text_part, swapped, quarter)
    text_grad_raw = backnorm(text_unit, text_radius, grad_text_emb)
    grad_image_emb = jnp.sum(image_sent.astype(F32), axis=0)
    image_grad_raw = backnorm(image_unit, image_radius, grad_image_emb)

    pieces = lax.all_gather(
        jnp.concatenate([image_grad_raw, text_grad_raw], axis=1), TENSOR, axis=0, tiled=True
    )
    piece_image, piece_text = pieces[:, :width], pieces[:, width:]

    def back(piece, proj):
        return lax.dot_general(
            piece, proj, (((1,), (1,)), ((), ())), preferred_element_type=F32
        ).astype(BF16)

    def outer(feats, piece):
        return lax.dot_general(feats, piece, (((0,), (0,)), ((), ())), preferred_element_type=F32)

    grad_image_w, grad_text_w = dp_sum(
        [outer(image_feats, piece_image), outer(text_feats, piece_text)]
    )
    return (
        back(piece_image, image_proj),
        back(piece_text, text_proj),
        grad_image_w,
        grad_text_w,
    )


def solution(mesh):
    fine = Mesh(mesh.devices.reshape(2, 8, 4, 2, 2), AXES)
    feats = P(("yhi", "z", "x"), TENSOR)
    proj = P(TENSOR, None)
    return jax.shard_map(
        per_device,
        mesh=fine,
        in_specs=(feats, feats, proj, proj),
        out_specs=(feats, feats, proj, proj),
        check_vma=False,
    )
```

```python
import jax
import jax.numpy as jnp
from jax import lax
from jax.sharding import Mesh, PartitionSpec as P

SCALE = 10.0
OFFSET = -4.0
EPSILON = 1e-06
F32 = jnp.float32
BF16 = jnp.bfloat16

AXES = ("yhi", "z", "x", "ylo", "core")
PLANE = ("yhi", "x", "ylo")
TENSOR = ("ylo", "core")
LANES = 128


def shift(value, axis, by):
    n = lax.axis_size(axis)
    return lax.ppermute(value, axis, [(i, (i + by) % n) for i in range(n)])


def flip(value, axis, bit):
    n = lax.axis_size(axis)
    return lax.ppermute(value, axis, [(i, i ^ bit) for i in range(n)])


def normalize(raw):
    radius = jnp.sqrt(jnp.sum(raw * raw, axis=1, keepdims=True) + EPSILON)
    return (raw / radius, radius)


def backnorm(unit, radius, grad):
    return ((grad - unit * jnp.sum(unit * grad, axis=1, keepdims=True)) / radius).astype(BF16)


def core_half(partial):
    core = lax.axis_index("core")
    rows, width = partial.shape
    parts = partial.reshape(2, 2, rows // 4, width)
    keep = lax.dynamic_index_in_dim(parts, core, 1, keepdims=False)
    send = lax.dynamic_index_in_dim(parts, 1 - core, 1, keepdims=False)
    return keep + flip(send.astype(BF16), "core", 1).astype(F32)


def quarter_rows(half):
    ylo = lax.axis_index("ylo")
    keep = lax.dynamic_index_in_dim(half, ylo, 0, keepdims=False)
    send = lax.dynamic_index_in_dim(half, 1 - ylo, 0, keepdims=False)
    return keep + flip(send.astype(BF16), "ylo", 1).astype(F32)


def column_shift(value, by):
    n = lax.axis_size("z")
    pairs = [(2 * z, (z + by) % n * 2) for z in range(n)]
    pairs += [(2 * z + 1, (z - by) % n * 2 + 1) for z in range(n)]
    return lax.ppermute(value, ("z", "core"), pairs)


def column_gather(value):
    first = lax.axis_index("core") == 0
    other = flip(value, "core", 1)
    pair = jnp.concatenate([jnp.where(first, value, other), jnp.where(first, other, value)], axis=0)
    rows = value.shape[0]
    got = {k: column_shift(pair, k) for k in (3, 2, 1)}
    far = column_shift(jnp.where(first, got[3][:rows], got[3][rows:]), 1)
    mine = lax.optimization_barrier(jnp.concatenate([got[1], got[2], got[3], far], axis=0))
    return jnp.concatenate([pair, mine, flip(mine, "core", 1)], axis=0)


def column_sum(parts, swapped, rows):
    first = lax.axis_index("core") == 0
    own = parts[: 2 * rows].astype(F32)

    def sent(start, stop):
        mine = parts[2 * rows + start : 2 * rows + stop].astype(F32)
        return (mine + swapped[start:stop].astype(F32)).astype(BF16)

    half = column_shift(sent(6 * rows, 7 * rows), -4).astype(F32)
    for k in (3, 2, 1):
        own = own + column_shift(sent(2 * rows * (k - 1), 2 * rows * k), -k).astype(F32)
    send = jnp.where(first, own[rows:], own[:rows]).astype(BF16)
    return jnp.where(first, own[:rows], own[rows:]) + half + flip(send, "core", 1).astype(F32)


def to_tiles(grad, pieces):
    rows, width = grad.shape
    count = rows * width // (8 * LANES)
    each = -(-count // pieces)
    tiles = grad.reshape(rows // 8, 8, width // LANES, LANES).transpose(0, 2, 1, 3)
    tiles = tiles.reshape(count, 8, LANES)
    tiles = jnp.pad(tiles, ((0, pieces * each - count), (0, 0), (0, 0)))
    return tiles.reshape(pieces, each * 8, LANES)


def from_tiles(tiles, rows, width):
    count = rows * width // (8 * LANES)
    tiles = tiles.reshape(-1, 8, LANES)[:count].reshape(rows // 8, width // LANES, 8, LANES)
    return tiles.transpose(0, 2, 1, 3).reshape(rows, width)


def column_scatter_sum(tiles):
    z, n = lax.axis_index("z"), lax.axis_size("z")
    sign = 1 - 2 * lax.axis_index("core")

    def block(k):
        return lax.dynamic_index_in_dim(tiles, (z + n + k) % n, 0, keepdims=False)

    away = jnp.stack([block(-sign * k) for k in (1, 2, 3)]).astype(BF16)
    got = flip(away, "core", 1)
    mine = block(0) + column_shift(block(4).astype(BF16), 4).astype(F32)
    pairs = {
        k: column_shift(jnp.stack([block(sign * k).astype(BF16), got[k - 1]]), k) for k in (3, 2, 1)
    }
    theirs = sum(pairs[k][1].astype(F32) for k in (1, 2, 3)).astype(BF16)
    mine = mine + sum(pairs[k][0].astype(F32) for k in (1, 2, 3))
    return mine + flip(theirs, "core", 1).astype(F32)


def column_spread(value):
    z, n = lax.axis_index("z"), lax.axis_size("z")
    first = lax.axis_index("core") == 0
    pair = jnp.stack([value, flip(value, "core", 1)])
    far = column_shift(value, 4)
    got = {k: column_shift(pair, k) for k in (3, 2, 1)}
    far, got = lax.optimization_barrier((far, got))
    swapped = flip(jnp.stack([got[k][1] for k in (1, 2, 3)]), "core", 1)
    above = [jnp.where(first, swapped[k - 1], got[k][0]) for k in (1, 2, 3)]
    below = [jnp.where(first, got[k][0], swapped[k - 1]) for k in (3, 2, 1)]
    ring = [value] + above + [far] + below
    return lax.dynamic_slice_in_dim(jnp.stack(ring + ring), (n - z) % n, n, 0)


def dp_sum(grads):
    x = lax.axis_index("x")
    rows, width = grads[0].shape
    unit = rows // 4
    half = (unit + 8) // 16 * 8

    def part(k):
        start = (x + k) % 4 * unit
        return jnp.stack([lax.dynamic_slice_in_dim(g, start, unit, 0) for g in grads])

    far = part(2).astype(BF16)
    up = shift(far[:, :half], "x", 1)
    down = shift(far[:, half:], "x", -1)
    right, left = part(1), part(3)
    up = jnp.concatenate([right[:, :half] + up.astype(F32), right[:, half:]], axis=1)
    down = jnp.concatenate([left[:, :half], left[:, half:] + down.astype(F32)], axis=1)
    up = shift(up.astype(BF16), "x", 1)
    down = shift(down.astype(BF16), "x", -1)
    mine = part(0) + up.astype(F32) + down.astype(F32)
    tiles = to_tiles(mine.reshape(2 * unit, width), lax.axis_size("z"))
    sent = column_scatter_sum(tiles).astype(BF16)
    total = (sent.astype(F32) + flip(sent, "yhi", 1).astype(F32)).astype(BF16)
    mine = from_tiles(column_spread(total), 2 * unit, width).reshape(2, unit, width)
    from_left = shift(mine, "x", 1)
    from_right = shift(mine, "x", -1)
    up = shift(from_left[:, :half], "x", 1)
    down = shift(from_right[:, half:], "x", -1)
    out = []
    for h in range(2):
        whole = jnp.zeros((rows, width), F32)
        far = jnp.concatenate([up[h], down[h]], axis=0)
        for k, value in enumerate((mine[h], from_right[h], far, from_left[h])):
            place = (x + k) % 4 * unit
            whole = lax.dynamic_update_slice_in_dim(whole, value.astype(F32), place, 0)
        out.append(whole)
    return out


def per_device(image_feats, text_feats, image_proj, text_proj):
    width = image_proj.shape[1]
    quarter = image_feats.shape[0] // 4
    plane = 16

    image_half = core_half(jnp.dot(image_feats, image_proj, preferred_element_type=F32))
    text_half = core_half(jnp.dot(text_feats, text_proj, preferred_element_type=F32))
    image_unit, image_radius = normalize(quarter_rows(image_half))
    text_unit, text_radius = normalize(quarter_rows(text_half))
    spread = jnp.broadcast_to(image_unit.astype(BF16)[None], (plane, quarter, width))
    spread, text_emb = lax.optimization_barrier((spread, text_unit.astype(BF16)))
    images = lax.all_to_all(spread, PLANE, 0, 0).reshape(-1, width)
    texts = column_gather(text_emb)
    own_image = lax.axis_index(PLANE) * quarter
    own_text = lax.axis_index("core") * quarter
    scores = lax.dot_general(images, texts, (((1,), (1,)), ((), ())), preferred_element_type=F32)
    row_id = lax.broadcasted_iota(jnp.int32, scores.shape, 0)
    col_id = lax.broadcasted_iota(jnp.int32, scores.shape, 1)
    own_id = col_id - own_text
    label = (row_id == own_id + own_image) & (own_id >= 0) & (own_id < quarter)
    weights = (SCALE * (jax.nn.sigmoid(SCALE * scores + OFFSET) - label.astype(F32))).astype(BF16)

    text_part = lax.dot_general(
        weights, images, (((0,), (0,)), ((), ())), preferred_element_type=F32
    ).astype(BF16)
    swapped = flip(text_part[9 * quarter :], "core", 1)
    weights, text_part = lax.optimization_barrier((weights, text_part))
    image_part = jnp.dot(weights, texts, preferred_element_type=F32).astype(BF16)
    image_part, swapped = lax.optimization_barrier((image_part, swapped))
    image_sent = lax.all_to_all(image_part.reshape(plane, quarter, width), PLANE, 0, 0)
    grad_text_emb = column_sum(text_part, swapped, quarter)
    text_grad_raw = backnorm(text_unit, text_radius, grad_text_emb)
    grad_image_emb = jnp.sum(image_sent.astype(F32), axis=0)
    image_grad_raw = backnorm(image_unit, image_radius, grad_image_emb)

    pieces = lax.all_gather(
        jnp.concatenate([image_grad_raw, text_grad_raw], axis=1), TENSOR, axis=0, tiled=True
    )
    piece_image, piece_text = pieces[:, :width], pieces[:, width:]

    def back(piece, proj):
        return lax.dot_general(
            piece, proj, (((1,), (1,)), ((), ())), preferred_element_type=F32
        ).astype(BF16)

    def outer(feats, piece):
        return lax.dot_general(feats, piece, (((0,), (0,)), ((), ())), preferred_element_type=F32)

    grad_image_w, grad_text_w = dp_sum(
        [outer(image_feats, piece_image), outer(text_feats, piece_text)]
    )
    return (
        back(piece_image, image_proj),
        back(piece_text, text_proj),
        grad_image_w,
        grad_text_w,
    )


def solution(mesh):
    fine = Mesh(mesh.devices.reshape(2, 8, 4, 2, 2), AXES)
    feats = P(("yhi", "z", "x"), TENSOR)
    proj = P(TENSOR, None)
    return jax.shard_map(
        per_device,
        mesh=fine,
        in_specs=(feats, feats, proj, proj),
        out_specs=(feats, feats, proj, proj),
        check_vma=False,
    )
```

```python
import jax
import jax.numpy as jnp
from jax import lax
from jax.sharding import Mesh, PartitionSpec as P

SCALE = 10.0
OFFSET = -4.0
EPSILON = 1e-06
F32 = jnp.float32
BF16 = jnp.bfloat16

AXES = ("yhi", "z", "x", "ylo", "core")
PLANE = ("yhi", "x", "ylo")
TENSOR = ("ylo", "core")
LANES = 128


def shift(value, axis, by):
    n = lax.axis_size(axis)
    return lax.ppermute(value, axis, [(i, (i + by) % n) for i in range(n)])


def flip(value, axis, bit):
    n = lax.axis_size(axis)
    return lax.ppermute(value, axis, [(i, i ^ bit) for i in range(n)])


def normalize(raw):
    radius = jnp.sqrt(jnp.sum(raw * raw, axis=1, keepdims=True) + EPSILON)
    return (raw / radius, radius)


def backnorm(unit, radius, grad):
    return ((grad - unit * jnp.sum(unit * grad, axis=1, keepdims=True)) / radius).astype(BF16)


def core_half(partial):
    core = lax.axis_index("core")
    rows, width = partial.shape
    parts = partial.reshape(2, 2, rows // 4, width)
    keep = lax.dynamic_index_in_dim(parts, core, 1, keepdims=False)
    send = lax.dynamic_index_in_dim(parts, 1 - core, 1, keepdims=False)
    return keep + flip(send.astype(BF16), "core", 1).astype(F32)


def quarter_rows(half):
    ylo = lax.axis_index("ylo")
    keep = lax.dynamic_index_in_dim(half, ylo, 0, keepdims=False)
    send = lax.dynamic_index_in_dim(half, 1 - ylo, 0, keepdims=False)
    return keep + flip(send.astype(BF16), "ylo", 1).astype(F32)


def column_shift(value, by):
    n = lax.axis_size("z")
    pairs = [(2 * z, (z + by) % n * 2) for z in range(n)]
    pairs += [(2 * z + 1, (z - by) % n * 2 + 1) for z in range(n)]
    return lax.ppermute(value, ("z", "core"), pairs)


def column_gather(value, images):
    first = lax.axis_index("core") == 0
    other = flip(value, "core", 1)
    pair = jnp.concatenate([jnp.where(first, value, other), jnp.where(first, other, value)], axis=0)
    rows = value.shape[0]
    got = {k: column_shift(pair, k) for k in (3, 2, 1)}
    far = column_shift(jnp.where(first, got[3][:rows], got[3][rows:]), 1)
    mine = lax.optimization_barrier(jnp.concatenate([got[1], got[2], got[3], far], axis=0))
    mine, images = lax.optimization_barrier((mine, images))
    return jnp.concatenate([pair, mine, flip(mine, "core", 1)], axis=0), images


def column_sum(parts, swapped, rows):
    first = lax.axis_index("core") == 0
    own = parts[: 2 * rows].astype(F32)

    def sent(start, stop):
        mine = parts[2 * rows + start : 2 * rows + stop].astype(F32)
        return (mine + swapped[start:stop].astype(F32)).astype(BF16)

    half = column_shift(sent(6 * rows, 7 * rows), -4).astype(F32)
    for k in (3, 2, 1):
        own = own + column_shift(sent(2 * rows * (k - 1), 2 * rows * k), -k).astype(F32)
    send = jnp.where(first, own[rows:], own[:rows]).astype(BF16)
    return jnp.where(first, own[:rows], own[rows:]) + half + flip(send, "core", 1).astype(F32)


def to_tiles(grad, pieces):
    rows, width = grad.shape
    count = rows * width // (8 * LANES)
    each = -(-count // pieces)
    tiles = grad.reshape(rows // 8, 8, width // LANES, LANES).transpose(0, 2, 1, 3)
    tiles = tiles.reshape(count, 8, LANES)
    tiles = jnp.pad(tiles, ((0, pieces * each - count), (0, 0), (0, 0)))
    return tiles.reshape(pieces, each * 8, LANES)


def from_tiles(tiles, rows, width):
    count = rows * width // (8 * LANES)
    tiles = tiles.reshape(-1, 8, LANES)[:count].reshape(rows // 8, width // LANES, 8, LANES)
    return tiles.transpose(0, 2, 1, 3).reshape(rows, width)


def column_scatter_sum(tiles):
    z, n = lax.axis_index("z"), lax.axis_size("z")
    sign = 1 - 2 * lax.axis_index("core")

    def block(k):
        return lax.dynamic_index_in_dim(tiles, (z + n + k) % n, 0, keepdims=False)

    away = jnp.stack([block(-sign * k) for k in (1, 2, 3)]).astype(BF16)
    got = flip(away, "core", 1)
    mine = block(0) + column_shift(block(4).astype(BF16), 4).astype(F32)
    pairs = {
        k: column_shift(jnp.stack([block(sign * k).astype(BF16), got[k - 1]]), k) for k in (3, 2, 1)
    }
    theirs = sum(pairs[k][1].astype(F32) for k in (1, 2, 3)).astype(BF16)
    mine = mine + sum(pairs[k][0].astype(F32) for k in (1, 2, 3))
    return mine + flip(theirs, "core", 1).astype(F32)


def column_spread(value):
    z, n = lax.axis_index("z"), lax.axis_size("z")
    first = lax.axis_index("core") == 0
    pair = jnp.stack([value, flip(value, "core", 1)])
    far = column_shift(value, 4)
    got = {k: column_shift(pair, k) for k in (3, 2, 1)}
    far, got = lax.optimization_barrier((far, got))
    swapped = flip(jnp.stack([got[k][1] for k in (1, 2, 3)]), "core", 1)
    above = [jnp.where(first, swapped[k - 1], got[k][0]) for k in (1, 2, 3)]
    below = [jnp.where(first, got[k][0], swapped[k - 1]) for k in (3, 2, 1)]
    ring = [value] + above + [far] + below
    return lax.dynamic_slice_in_dim(jnp.stack(ring + ring), (n - z) % n, n, 0)


def dp_sum(grads):
    x = lax.axis_index("x")
    rows, width = grads[0].shape
    unit = rows // 4
    half = (unit + 8) // 16 * 8

    def part(k):
        start = (x + k) % 4 * unit
        return jnp.stack([lax.dynamic_slice_in_dim(g, start, unit, 0) for g in grads])

    far = part(2).astype(BF16)
    up = shift(far[:, :half], "x", 1)
    down = shift(far[:, half:], "x", -1)
    right, left = part(1), part(3)
    up = jnp.concatenate([right[:, :half] + up.astype(F32), right[:, half:]], axis=1)
    down = jnp.concatenate([left[:, :half], left[:, half:] + down.astype(F32)], axis=1)
    up = shift(up.astype(BF16), "x", 1)
    down = shift(down.astype(BF16), "x", -1)
    mine = part(0) + up.astype(F32) + down.astype(F32)
    tiles = to_tiles(mine.reshape(2 * unit, width), lax.axis_size("z"))
    sent = column_scatter_sum(tiles).astype(BF16)
    total = (sent.astype(F32) + flip(sent, "yhi", 1).astype(F32)).astype(BF16)
    mine = from_tiles(column_spread(total), 2 * unit, width).reshape(2, unit, width)
    from_left = shift(mine, "x", 1)
    from_right = shift(mine, "x", -1)
    up = shift(from_left[:, :half], "x", 1)
    down = shift(from_right[:, half:], "x", -1)
    out = []
    for h in range(2):
        whole = jnp.zeros((rows, width), F32)
        far = jnp.concatenate([up[h], down[h]], axis=0)
        for k, value in enumerate((mine[h], from_right[h], far, from_left[h])):
            place = (x + k) % 4 * unit
            whole = lax.dynamic_update_slice_in_dim(whole, value.astype(F32), place, 0)
        out.append(whole)
    return out


def per_device(image_feats, text_feats, image_proj, text_proj):
    width = image_proj.shape[1]
    quarter = image_feats.shape[0] // 4
    plane = 16

    image_half = core_half(jnp.dot(image_feats, image_proj, preferred_element_type=F32))
    text_half = core_half(jnp.dot(text_feats, text_proj, preferred_element_type=F32))
    image_unit, image_radius = normalize(quarter_rows(image_half))
    text_unit, text_radius = normalize(quarter_rows(text_half))
    spread = jnp.broadcast_to(image_unit.astype(BF16)[None], (plane, quarter, width))
    spread, text_emb = lax.optimization_barrier((spread, text_unit.astype(BF16)))
    images = lax.all_to_all(spread, PLANE, 0, 0).reshape(-1, width)
    texts, images = column_gather(text_emb, images)
    own_image = lax.axis_index(PLANE) * quarter
    own_text = lax.axis_index("core") * quarter
    scores = lax.dot_general(images, texts, (((1,), (1,)), ((), ())), preferred_element_type=F32)
    row_id = lax.broadcasted_iota(jnp.int32, scores.shape, 0)
    col_id = lax.broadcasted_iota(jnp.int32, scores.shape, 1)
    own_id = col_id - own_text
    label = (row_id == own_id + own_image) & (own_id >= 0) & (own_id < quarter)
    weights = (SCALE * (jax.nn.sigmoid(SCALE * scores + OFFSET) - label.astype(F32))).astype(BF16)

    text_part = lax.dot_general(
        weights, images, (((0,), (0,)), ((), ())), preferred_element_type=F32
    ).astype(BF16)
    swapped = flip(text_part[9 * quarter :], "core", 1)
    weights, text_part = lax.optimization_barrier((weights, text_part))
    image_part = jnp.dot(weights, texts, preferred_element_type=F32).astype(BF16)
    image_part, swapped = lax.optimization_barrier((image_part, swapped))
    image_sent = lax.all_to_all(image_part.reshape(plane, quarter, width), PLANE, 0, 0)
    grad_text_emb = column_sum(text_part, swapped, quarter)
    text_grad_raw = backnorm(text_unit, text_radius, grad_text_emb)
    grad_image_emb = jnp.sum(image_sent.astype(F32), axis=0)
    image_grad_raw = backnorm(image_unit, image_radius, grad_image_emb)

    pieces = lax.all_gather(
        jnp.concatenate([image_grad_raw, text_grad_raw], axis=1), TENSOR, axis=0, tiled=True
    )
    piece_image, piece_text = pieces[:, :width], pieces[:, width:]

    def back(piece, proj):
        return lax.dot_general(
            piece, proj, (((1,), (1,)), ((), ())), preferred_element_type=F32
        ).astype(BF16)

    def outer(feats, piece):
        return lax.dot_general(feats, piece, (((0,), (0,)), ((), ())), preferred_element_type=F32)

    grad_image_w, grad_text_w = dp_sum(
        [outer(image_feats, piece_image), outer(text_feats, piece_text)]
    )
    return (
        back(piece_image, image_proj),
        back(piece_text, text_proj),
        grad_image_w,
        grad_text_w,
    )


def solution(mesh):
    fine = Mesh(mesh.devices.reshape(2, 8, 4, 2, 2), AXES)
    feats = P(("yhi", "z", "x"), TENSOR)
    proj = P(TENSOR, None)
    return jax.shard_map(
        per_device,
        mesh=fine,
        in_specs=(feats, feats, proj, proj),
        out_specs=(feats, feats, proj, proj),
        check_vma=False,
    )
```

```python
import jax
import jax.numpy as jnp
from jax import lax
from jax.sharding import Mesh, PartitionSpec as P

SCALE = 10.0
OFFSET = -4.0
EPSILON = 1e-06
F32 = jnp.float32
BF16 = jnp.bfloat16

AXES = ("yhi", "z", "x", "ylo", "core")
PLANE = ("yhi", "x", "ylo")
TENSOR = ("ylo", "core")
LANES = 128


def shift(value, axis, by):
    n = lax.axis_size(axis)
    return lax.ppermute(value, axis, [(i, (i + by) % n) for i in range(n)])


def flip(value, axis, bit):
    n = lax.axis_size(axis)
    return lax.ppermute(value, axis, [(i, i ^ bit) for i in range(n)])


def normalize(raw):
    radius = jnp.sqrt(jnp.sum(raw * raw, axis=1, keepdims=True) + EPSILON)
    return (raw / radius, radius)


def backnorm(unit, radius, grad):
    return ((grad - unit * jnp.sum(unit * grad, axis=1, keepdims=True)) / radius).astype(BF16)


def core_half(partial):
    core = lax.axis_index("core")
    rows, width = partial.shape
    parts = partial.reshape(2, 2, rows // 4, width)
    keep = lax.dynamic_index_in_dim(parts, core, 1, keepdims=False)
    send = lax.dynamic_index_in_dim(parts, 1 - core, 1, keepdims=False)
    return keep + flip(send.astype(BF16), "core", 1).astype(F32)


def quarter_rows(half):
    ylo = lax.axis_index("ylo")
    keep = lax.dynamic_index_in_dim(half, ylo, 0, keepdims=False)
    send = lax.dynamic_index_in_dim(half, 1 - ylo, 0, keepdims=False)
    return keep + flip(send.astype(BF16), "ylo", 1).astype(F32)


def column_shift(value, by):
    n = lax.axis_size("z")
    pairs = [(2 * z, (z + by) % n * 2) for z in range(n)]
    pairs += [(2 * z + 1, (z - by) % n * 2 + 1) for z in range(n)]
    return lax.ppermute(value, ("z", "core"), pairs)


def column_gather(value, images):
    first = lax.axis_index("core") == 0
    other = flip(value, "core", 1)
    pair = jnp.concatenate([jnp.where(first, value, other), jnp.where(first, other, value)], axis=0)
    rows = value.shape[0]
    got = {k: column_shift(pair, k) for k in (3, 2, 1)}
    far = column_shift(jnp.where(first, got[3][:rows], got[3][rows:]), 1)
    mine = lax.optimization_barrier(jnp.concatenate([got[1], got[2], got[3], far], axis=0))
    mine, images = lax.optimization_barrier((mine, images))
    return jnp.concatenate([pair, mine, flip(mine, "core", 1)], axis=0), images


def column_sum(parts, swapped, rows, image_sent):
    first = lax.axis_index("core") == 0
    own = parts[: 2 * rows].astype(F32)

    def sent(start, stop):
        mine = parts[2 * rows + start : 2 * rows + stop].astype(F32)
        return (mine + swapped[start:stop].astype(F32)).astype(BF16)

    relay = column_shift(sent(6 * rows, 7 * rows), -1)
    none = jnp.zeros_like(relay)
    relay = jnp.concatenate([jnp.where(first, relay, none), jnp.where(first, none, relay)], axis=0)
    last = parts[6 * rows : 8 * rows].astype(F32) + swapped[4 * rows : 6 * rows].astype(F32)
    last = (last + relay.astype(F32)).astype(BF16)
    own = own + column_shift(last, -3).astype(F32)
    for k in (2, 1):
        own = own + column_shift(sent(2 * rows * (k - 1), 2 * rows * k), -k).astype(F32)
    own, image_sent = lax.optimization_barrier((own, image_sent))
    send = jnp.where(first, own[rows:], own[:rows]).astype(BF16)
    return jnp.where(first, own[:rows], own[rows:]) + flip(send, "core", 1).astype(F32), image_sent


def to_tiles(grad, pieces):
    rows, width = grad.shape
    count = rows * width // (8 * LANES)
    each = -(-count // pieces)
    tiles = grad.reshape(rows // 8, 8, width // LANES, LANES).transpose(0, 2, 1, 3)
    tiles = tiles.reshape(count, 8, LANES)
    tiles = jnp.pad(tiles, ((0, pieces * each - count), (0, 0), (0, 0)))
    return tiles.reshape(pieces, each * 8, LANES)


def from_tiles(tiles, rows, width):
    count = rows * width // (8 * LANES)
    tiles = tiles.reshape(-1, 8, LANES)[:count].reshape(rows // 8, width // LANES, 8, LANES)
    return tiles.transpose(0, 2, 1, 3).reshape(rows, width)


def column_scatter_sum(tiles):
    z, n = lax.axis_index("z"), lax.axis_size("z")
    sign = 1 - 2 * lax.axis_index("core")

    def block(k):
        return lax.dynamic_index_in_dim(tiles, (z + n + k) % n, 0, keepdims=False)

    away = jnp.stack([block(-sign * k) for k in (1, 2, 3)]).astype(BF16)
    got = flip(away, "core", 1)
    mine = block(0) + column_shift(block(4).astype(BF16), 4).astype(F32)
    pairs = {
        k: column_shift(jnp.stack([block(sign * k).astype(BF16), got[k - 1]]), k) for k in (3, 2, 1)
    }
    theirs = sum(pairs[k][1].astype(F32) for k in (1, 2, 3)).astype(BF16)
    mine = mine + sum(pairs[k][0].astype(F32) for k in (1, 2, 3))
    return mine + flip(theirs, "core", 1).astype(F32)


def column_spread(value):
    z, n = lax.axis_index("z"), lax.axis_size("z")
    first = lax.axis_index("core") == 0
    pair = jnp.stack([value, flip(value, "core", 1)])
    far = column_shift(value, 4)
    got = {k: column_shift(pair, k) for k in (3, 2, 1)}
    far, got = lax.optimization_barrier((far, got))
    swapped = flip(jnp.stack([got[k][1] for k in (1, 2, 3)]), "core", 1)
    above = [jnp.where(first, swapped[k - 1], got[k][0]) for k in (1, 2, 3)]
    below = [jnp.where(first, got[k][0], swapped[k - 1]) for k in (3, 2, 1)]
    ring = [value] + above + [far] + below
    return lax.dynamic_slice_in_dim(jnp.stack(ring + ring), (n - z) % n, n, 0)


def dp_sum(grads):
    x = lax.axis_index("x")
    rows, width = grads[0].shape
    unit = rows // 4
    half = (unit + 8) // 16 * 8

    def part(k):
        start = (x + k) % 4 * unit
        return jnp.stack([lax.dynamic_slice_in_dim(g, start, unit, 0) for g in grads])

    far = part(2).astype(BF16)
    up = shift(far[:, :half], "x", 1)
    down = shift(far[:, half:], "x", -1)
    right, left = part(1), part(3)
    up = jnp.concatenate([right[:, :half] + up.astype(F32), right[:, half:]], axis=1)
    down = jnp.concatenate([left[:, :half], left[:, half:] + down.astype(F32)], axis=1)
    up = shift(up.astype(BF16), "x", 1)
    down = shift(down.astype(BF16), "x", -1)
    mine = part(0) + up.astype(F32) + down.astype(F32)
    tiles = to_tiles(mine.reshape(2 * unit, width), lax.axis_size("z"))
    sent = column_scatter_sum(tiles).astype(BF16)
    total = (sent.astype(F32) + flip(sent, "yhi", 1).astype(F32)).astype(BF16)
    mine = from_tiles(column_spread(total), 2 * unit, width).reshape(2, unit, width)
    from_left = shift(mine, "x", 1)
    from_right = shift(mine, "x", -1)
    up = shift(from_left[:, :half], "x", 1)
    down = shift(from_right[:, half:], "x", -1)
    out = []
    for h in range(2):
        whole = jnp.zeros((rows, width), F32)
        far = jnp.concatenate([up[h], down[h]], axis=0)
        for k, value in enumerate((mine[h], from_right[h], far, from_left[h])):
            place = (x + k) % 4 * unit
            whole = lax.dynamic_update_slice_in_dim(whole, value.astype(F32), place, 0)
        out.append(whole)
    return out


def per_device(image_feats, text_feats, image_proj, text_proj):
    width = image_proj.shape[1]
    quarter = image_feats.shape[0] // 4
    plane = 16

    image_half = core_half(jnp.dot(image_feats, image_proj, preferred_element_type=F32))
    text_half = core_half(jnp.dot(text_feats, text_proj, preferred_element_type=F32))
    image_unit, image_radius = normalize(quarter_rows(image_half))
    text_unit, text_radius = normalize(quarter_rows(text_half))
    spread = jnp.broadcast_to(image_unit.astype(BF16)[None], (plane, quarter, width))
    spread, text_emb = lax.optimization_barrier((spread, text_unit.astype(BF16)))
    images = lax.all_to_all(spread, PLANE, 0, 0).reshape(-1, width)
    texts, images = column_gather(text_emb, images)
    own_image = lax.axis_index(PLANE) * quarter
    own_text = lax.axis_index("core") * quarter
    scores = lax.dot_general(images, texts, (((1,), (1,)), ((), ())), preferred_element_type=F32)
    row_id = lax.broadcasted_iota(jnp.int32, scores.shape, 0)
    col_id = lax.broadcasted_iota(jnp.int32, scores.shape, 1)
    own_id = col_id - own_text
    label = (row_id == own_id + own_image) & (own_id >= 0) & (own_id < quarter)
    weights = (SCALE * (jax.nn.sigmoid(SCALE * scores + OFFSET) - label.astype(F32))).astype(BF16)

    text_part = lax.dot_general(
        weights, images, (((0,), (0,)), ((), ())), preferred_element_type=F32
    ).astype(BF16)
    swapped = flip(text_part[9 * quarter :], "core", 1)
    weights, text_part = lax.optimization_barrier((weights, text_part))
    image_part = jnp.dot(weights, texts, preferred_element_type=F32).astype(BF16)
    image_part, swapped = lax.optimization_barrier((image_part, swapped))
    image_sent = lax.all_to_all(image_part.reshape(plane, quarter, width), PLANE, 0, 0)
    grad_text_emb, image_sent = column_sum(text_part, swapped, quarter, image_sent)
    text_grad_raw = backnorm(text_unit, text_radius, grad_text_emb)
    grad_image_emb = jnp.sum(image_sent.astype(F32), axis=0)
    image_grad_raw = backnorm(image_unit, image_radius, grad_image_emb)

    pieces = lax.all_gather(
        jnp.concatenate([image_grad_raw, text_grad_raw], axis=1), TENSOR, axis=0, tiled=True
    )
    piece_image, piece_text = pieces[:, :width], pieces[:, width:]

    def back(piece, proj):
        return lax.dot_general(
            piece, proj, (((1,), (1,)), ((), ())), preferred_element_type=F32
        ).astype(BF16)

    def outer(feats, piece):
        return lax.dot_general(feats, piece, (((0,), (0,)), ((), ())), preferred_element_type=F32)

    grad_image_w, grad_text_w = dp_sum(
        [outer(image_feats, piece_image), outer(text_feats, piece_text)]
    )
    return (
        back(piece_image, image_proj),
        back(piece_text, text_proj),
        grad_image_w,
        grad_text_w,
    )


def solution(mesh):
    fine = Mesh(mesh.devices.reshape(2, 8, 4, 2, 2), AXES)
    feats = P(("yhi", "z", "x"), TENSOR)
    proj = P(TENSOR, None)
    return jax.shard_map(
        per_device,
        mesh=fine,
        in_specs=(feats, feats, proj, proj),
        out_specs=(feats, feats, proj, proj),
        check_vma=False,
    )
```
